128 devices in a mesh: front: 4 (over y), sub: 32 (over x, z, core).
Axes of the slice: x: 4, y: 4, z: 4, core: 2. Of those that a mesh axis runs over, the one named last changes fastest.
Arguments:
- front: float32 [16, 4096, 2048], P('front', 'sub'), parts along dimension 0, may hold values from -8 to 1208
- children: float32 [24, 4096, 2048], P('front', 'sub'), parts along dimension 0, may hold values from -0.5 to 0.5
- row_maps: int32 [8, 96], P('front'), parts along dimension 0, may hold values from 0 to 127, as said below
Outputs:
- panel: float32 [16, 4096, 256], P('front', 'sub'), parts along dimension 0
- update: float32 [16, 4096, 1792], P('front', 'sub'), parts along dimension 0
The draws below stay inside these ranges and needn't reach their ends.
There are 4 independent parts, one for each index of `front`. The reference program is written for one: setup_inputs(seed, part) draws one part's arguments, and reference() takes and returns one part's arrays. A program takes and returns all parts, laid end to end along the dimension named above; each array names one. Nothing has to cross between parts.
Inputs may be any that keep to these rules, and one draw needn't show every extreme that they name: row_maps[k, b] and b agree modulo 16; the entries of one child are distinct; for each residue i below 16 each child has exactly one block mapped to i and one mapped to i + 16; among each child's blocks of one residue exactly 3 are mapped to blocks p with p // 16 even.
All inputs are finite; a program needn't handle non-finite values.
Results may differ from the reference program's by a relative error of at most 0.00009.
Values sent between devices are 32-bit elements; how exact they have to be, the bound alone decides.
No kernel may reach another device: no remote copies, remote signals or barrier semaphores. Data moves between devices by JAX's collectives and lax.ppermute only.
A program may use at most 128 MiB of HBM per device.

```python
import jax
import jax.numpy as jnp
from jax import lax

F = 16384
BLK = 128
PANEL = 256
W = 2048
PSLOT = 4
CSLOT = 6
NPB = 128
NCB = 96
N_SUB = 32


def draw_front(key, part):
    key = jax.random.fold_in(key, 11)
    key_one = jax.random.fold_in(key, 0)
    key_three = jax.random.fold_in(key, 2)
    shape = (PSLOT, N_SUB * BLK, W)
    rows = jnp.arange(PSLOT)[:, None, None] * (N_SUB * BLK) + jnp.arange(N_SUB * BLK)[None, :, None]
    columns = jnp.arange(W)[None, None, :]
    values = jax.random.uniform(key_one, shape, minval=-1.0, maxval=1.0)
    values = jnp.where((columns < PANEL) & (rows >= PANEL), 8.0 * values, values)
    boost = jax.random.uniform(key_three, shape, minval=600.0, maxval=1200.0)
    values = jnp.where((rows == columns) & (columns < PANEL), values + boost, values)
    return values.astype(jnp.float32)


def draw_children(key, part):
    key = jax.random.fold_in(key, 23)
    key_one = jax.random.fold_in(key, 0)
    shape = (CSLOT, N_SUB * BLK, W)
    values = 0.5 * jax.random.uniform(key_one, shape, minval=-1.0, maxval=1.0)
    return values.astype(jnp.float32)


def random_order(key, count):
    scores = jax.random.randint(key, (count,), 0, 1 << 30)
    return jnp.argsort(scores, stable=True).astype(jnp.int32)


def draw_row_maps(key, part):
    key = jax.random.fold_in(key, 37)
    half_size = N_SUB // 2
    extra = CSLOT // 2 - 1

    def one_residue(sub_key):
        key_even, key_odd, key_mix = jax.random.split(sub_key, 3)
        even_picks = 2 * (1 + random_order(key_even, PSLOT - 1)[:extra])
        odd_picks = 1 + 2 * (1 + random_order(key_odd, PSLOT - 2)[:extra - 1])
        picks = jnp.concatenate([jnp.zeros((1,), jnp.int32), even_picks, jnp.ones((1,), jnp.int32), jnp.full((1,), 2 * PSLOT - 1, jnp.int32), odd_picks])
        return picks[random_order(key_mix, CSLOT)]
    keys = jax.random.split(key, 2 * half_size)
    picks = jax.vmap(one_residue)(keys).reshape(2, half_size, CSLOT)
    residues = jnp.arange(half_size, dtype=jnp.int32)[None, :, None]
    targets = residues + half_size * picks
    return targets.transpose(0, 2, 1).reshape(2, NCB).astype(jnp.int32)


def setup_inputs(seed: int = 0, part: int = 0) -> dict:
    seeds = jax.random.split(jax.random.key(seed), 4)
    part_splits = jax.random.split(jax.random.fold_in(seeds[3], part), 4)
    return {
        "front": draw_front(jax.random.fold_in(jax.random.fold_in(seeds[3], part), 71), part),
        "children": draw_children(jax.random.fold_in(jax.random.fold_in(seeds[3], part), 71), part),
        "row_maps": draw_row_maps(jax.random.fold_in(jax.random.fold_in(seeds[3], part), 71), part),
    }


def reference(front, children, row_maps):
    half_size = N_SUB // 2
    parent = front.reshape(NPB, BLK, W)
    blocks = children.reshape(CSLOT, 2, half_size, BLK, W).transpose(1, 0, 2, 3, 4).reshape(2, NCB, BLK, W)
    for which_child in range(2):
        parent = parent.at[row_maps[which_child]].add(blocks[which_child])
    assembled = parent.reshape(F, W)
    diag_block = assembled[:PANEL, :PANEL]
    lower_factor = jnp.linalg.cholesky(0.5 * (diag_block + diag_block.T))
    panel_full = jax.scipy.linalg.solve_triangular(lower_factor, assembled[:, :PANEL].T, lower=True).T
    update = assembled[:, PANEL:] - jnp.dot(panel_full, panel_full[PANEL:W].T, precision=lax.Precision.HIGHEST)
    return (panel_full.reshape(PSLOT, N_SUB * BLK, PANEL), update.reshape(PSLOT, N_SUB * BLK, W - PANEL))
```

```python
import functools

import jax
import jax.numpy as jnp
from jax import lax
from jax.experimental import pallas as pl
from jax.experimental.pallas import tpu as pltpu
from jax.sharding import PartitionSpec as P

PANEL = 256
BLK = 128
HIGHEST = lax.Precision.HIGHEST
VMEM_LIMIT = 60 << 20
GROUP = 64

OUT = 0
SLOT = 4
KEEP = 8
CAME = 12
SMALL = pl.CostEstimate(flops=0, bytes_accessed=0, transcendentals=0)


def matmul(a, b, ca, cb):
    return lax.dot_general(
        a, b, (((ca,), (cb,)), ((), ())), precision=HIGHEST, preferred_element_type=jnp.float32
    )


def any_space():
    return pl.BlockSpec(memory_space=pl.ANY)


def smem_space():
    return pl.BlockSpec(memory_space=pltpu.SMEM)


def params():
    return pltpu.CompilerParams(vmem_limit_bytes=VMEM_LIMIT)


def index_kernel(
    half, slots, maps, front, children, idx, piece, rest, others, base, mine, theirs, old, kept, sem
):
    dev = lax.axis_index("sub")
    sib = dev // half
    res = dev % half
    lead = pl.ds(0, PANEL)
    first = pltpu.make_async_copy(front.at[0, :, lead], old, sem.at[0])
    first.start()
    for step in range(8):
        mine[step] = -1
        theirs[step] = -1
    for b in range(slots):
        mine[(maps[sib, b * half + res] - res) // half] = b
        theirs[(maps[1 - sib, b * half + res] - res) // half] = b
    for i in range(16):
        idx[i] = -1
    n_out = jnp.int32(0)
    n_in = jnp.int32(0)
    none = jnp.int32(0)
    for q in range(4):
        b = mine[2 * q + 1 - sib]
        idx[OUT + n_out] = jnp.maximum(b, 0)
        n_out = n_out + jnp.where(b >= 0, 1, 0)
        idx[KEEP + q] = mine[2 * q + sib]
        t = theirs[2 * q + sib]
        idx[SLOT + n_in] = q
        idx[CAME + q] = jnp.where(t >= 0, n_in, -1)
        n_in = n_in + jnp.where(t >= 0, 1, 0)
        none = jnp.where(t >= 0, none, q)
    idx[SLOT + 3] = none
    keep = idx[KEEP]
    copies = [
        pltpu.make_async_copy(children.at[idx[OUT], :, lead], piece, sem.at[1]),
        pltpu.make_async_copy(children.at[jnp.maximum(keep, 0), :, lead], kept, sem.at[2]),
        pltpu.make_async_copy(
            children.at[idx[OUT], :, pl.ds(PANEL, rest.shape[1])], rest, sem.at[3]
        ),
        pltpu.make_async_copy(children.at[idx[OUT + 1], :, lead], others.at[0], sem.at[4]),
        pltpu.make_async_copy(children.at[idx[OUT + 2], :, lead], others.at[1], sem.at[5]),
    ]
    for copy in copies:
        copy.start()
    first.wait()
    for copy in copies:
        copy.wait()
    base[...] = old[...] + kept[...] * jnp.where(keep >= 0, 1.0, 0.0)


def make_indices(row_maps, front, children, half):
    rest = children.shape[2] - PANEL
    vmem = pl.BlockSpec(memory_space=pltpu.VMEM)
    return pl.pallas_call(
        functools.partial(index_kernel, half, children.shape[0]),
        name="indices",
        out_shape=(
            jax.ShapeDtypeStruct((16,), jnp.int32),
            jax.ShapeDtypeStruct((BLK, PANEL), jnp.float32),
            jax.ShapeDtypeStruct((BLK, rest), jnp.float32),
            jax.ShapeDtypeStruct((2, BLK, PANEL), jnp.float32),
            jax.ShapeDtypeStruct((BLK, PANEL), jnp.float32),
        ),
        in_specs=[smem_space(), any_space(), any_space()],
        out_specs=(smem_space(), vmem, vmem, vmem, vmem),
        scratch_shapes=[
            pltpu.SMEM((8,), jnp.int32),
            pltpu.SMEM((8,), jnp.int32),
            pltpu.VMEM((BLK, PANEL), jnp.float32),
            pltpu.VMEM((BLK, PANEL), jnp.float32),
            pltpu.SemaphoreType.DMA((6,)),
        ],
        compiler_params=params(),
        cost_estimate=SMALL,
    )(row_maps, front, children)


def take_kernel(idx, children, one, two, sem):
    part = pl.ds(PANEL, one.shape[1])
    copies = [
        pltpu.make_async_copy(children.at[idx[OUT + 1 + i], :, part], out, sem.at[i])
        for i, out in enumerate((one, two))
    ]
    for copy in copies:
        copy.start()
    for copy in copies:
        copy.wait()


def take_blocks(idx, children):
    shape = jax.ShapeDtypeStruct((BLK, children.shape[2] - PANEL), jnp.float32)
    vmem = pl.BlockSpec(memory_space=pltpu.VMEM)
    return pl.pallas_call(
        take_kernel,
        name="take",
        out_shape=(shape, shape),
        in_specs=[smem_space(), any_space()],
        out_specs=(vmem, vmem),
        scratch_shapes=[pltpu.SemaphoreType.DMA((2,))],
        compiler_params=params(),
        cost_estimate=SMALL,
    )(idx, children)


def inverse_factor(d):
    n = d.shape[0]
    row = lax.broadcasted_iota(jnp.int32, (n, n), 0)
    col = lax.broadcasted_iota(jnp.int32, (n, n), 1)
    m = jnp.concatenate([d, (row == col).astype(jnp.float32)], axis=1)
    w = 2 * n
    parts = n // 8
    groups = [m[8 * i : 8 * i + 8, :] for i in range(parts)]
    sub = lax.broadcasted_iota(jnp.int32, (8, w), 0)
    for q in range(parts):
        e = [
            [
                jnp.broadcast_to(groups[i][:, 8 * q + k : 8 * q + k + 1], (8, w))
                for i in range(q, parts)
            ]
            for k in range(8)
        ]
        for k in range(8):
            r = lax.rsqrt(jnp.broadcast_to(e[k][0][k : k + 1, :], (8, w)))
            pivot_row = jnp.broadcast_to(groups[q][k : k + 1, :], (8, w)) * r
            scaled = [v * r for v in e[k]]
            for i in range(q, parts):
                t = groups[i] - scaled[i - q] * pivot_row
                if i == q:
                    t = jnp.where(sub == k, pivot_row, jnp.where(sub > k, t, groups[i]))
                groups[i] = t
            for c in range(k + 1, 8):
                head = jnp.broadcast_to(e[c][0][k : k + 1, :], (8, w)) * r
                e[c] = [v - u * head for v, u in zip(e[c], scaled)]
    return jnp.concatenate(groups, axis=0)[:, n:]


def factor_kernel(half, *refs):
    pieces, (inv, wide), (window, m) = refs[:8], refs[8:10], refs[10:]
    dev = lax.axis_index("sub")
    z = (dev // 2) % 4
    core = dev % 2
    for i, ref in enumerate(pieces):
        zz = (z + i // 2) % 4
        cc = (core + i) % 2
        for h in range(2):
            block = (h * 4 + zz) * 2 + cc
            window[pl.ds(pl.multiple_of(block * BLK, BLK), BLK), :] = ref[h]
    s = window[0:PANEL, :]
    s = 0.5 * (s + s.T)
    m[:, :PANEL] = s
    row = lax.broadcasted_iota(jnp.int32, (PANEL, PANEL), 0)
    col = lax.broadcasted_iota(jnp.int32, (PANEL, PANEL), 1)
    m[:, PANEL:] = (row == col).astype(jnp.float32)
    for k in range(PANEL // GROUP):
        a, b = k * GROUP, (k + 1) * GROUP
        r = m[a:b, :]
        x = matmul(inverse_factor(r[:, a:b]), r, 1, 0)
        m[a:b, :] = x
        if b < PANEL:
            m[b:, :] = m[b:, :] - matmul(x[:, b:PANEL], x, 0, 0)
    linv = m[:, PANEL:]
    inv[...] = linv
    wide[...] = matmul(window[PANEL:, :], linv, 1, 1)


def factor(pieces, half, columns):
    return pl.pallas_call(
        functools.partial(factor_kernel, half),
        name="factor",
        out_shape=(
            jax.ShapeDtypeStruct((PANEL, PANEL), jnp.float32),
            jax.ShapeDtypeStruct((columns - PANEL, PANEL), jnp.float32),
        ),
        scratch_shapes=[
            pltpu.VMEM((columns, PANEL), jnp.float32),
            pltpu.VMEM((PANEL, 2 * PANEL), jnp.float32),
        ],
        compiler_params=params(),
        cost_estimate=SMALL,
    )(*pieces)


def base_kernel(slots, idx, *refs):
    fronts, (lead_front,), refs = refs[:1], refs[1:2], refs[2:]
    kept, lead_kept, (came, others, inv, wide, panel, update, held) = (
        refs[:slots], refs[slots : 2 * slots], refs[2 * slots :]
    )
    has = [jnp.where(idx[KEEP + q] >= 0, 1.0, 0.0) for q in range(slots)]

    @pl.when(pl.program_id(0) == 0)
    def _():
        for q in range(slots):
            which = idx[CAME + q]
            second = others[jnp.clip(which - 1, 0, 1)]
            got = jnp.where(which == 0, came[...], jnp.where(which > 0, second, 0.0))
            held[q * BLK : (q + 1) * BLK, :] = (
                lead_front[q] + lead_kept[q][0] * has[q] + got
            )
        p = matmul(held[...], inv[...], 1, 1)
        held[...] = p
        for q in range(slots):
            panel[q] = p[q * BLK : (q + 1) * BLK, :]

    u = matmul(held[...], wide[...], 1, 1)
    for q in range(slots):
        update[q] = fronts[0][q] + kept[q][0] * has[q] - u[q * BLK : (q + 1) * BLK, :]


def make_base(idx, front, children, came, others, inv, wide):
    slots, rows, columns = front.shape
    rest = columns - PANEL
    whole = lambda shape: pl.BlockSpec(shape, lambda i, idx: (0,) * len(shape))
    kept = lambda q, at: pl.BlockSpec(
        (1, rows, PANEL), lambda i, idx: (jnp.maximum(idx[KEEP + q], 0), 0, (i + 1) * at)
    )
    in_specs = (
        [
            pl.BlockSpec((slots, rows, PANEL), lambda i, idx: (0, 0, i + 1)),
            pl.BlockSpec((slots, rows, PANEL), lambda i, idx: (0, 0, 0)),
        ]
        + [kept(q, 1) for q in range(slots)]
        + [kept(q, 0) for q in range(slots)]
        + [
            whole(came.shape),
            whole(others.shape),
            whole(inv.shape),
            pl.BlockSpec((PANEL, PANEL), lambda i, idx: (i, 0)),
        ]
    )
    grid = pltpu.PrefetchScalarGridSpec(
        num_scalar_prefetch=1,
        grid=(rest // PANEL,),
        in_specs=in_specs,
        out_specs=(
            whole((slots, rows, PANEL)),
            pl.BlockSpec((slots, rows, PANEL), lambda i, idx: (0, 0, i)),
        ),
        scratch_shapes=[pltpu.VMEM((slots * rows, PANEL), jnp.float32)],
    )
    return pl.pallas_call(
        functools.partial(base_kernel, slots),
        name="base",
        out_shape=(
            jax.ShapeDtypeStruct((slots, rows, PANEL), jnp.float32),
            jax.ShapeDtypeStruct((slots, rows, rest), jnp.float32),
        ),
        grid_spec=grid,
        compiler_params=params(),
        cost_estimate=SMALL,
    )(idx, *[front] * 2, *[children] * (2 * slots), came, others, inv, wide)


def add_kernel(idx, old, came, out):
    out[0] = old[0] + came[...]


def add_block(idx, update, came, which):
    slots, rows, rest = update.shape
    at_slot = pl.BlockSpec((1, rows, rest), lambda i, idx: (idx[SLOT + which], 0, 0))
    grid = pltpu.PrefetchScalarGridSpec(
        num_scalar_prefetch=1,
        grid=(1,),
        in_specs=[at_slot, pl.BlockSpec(came.shape, lambda i, idx: (0, 0))],
        out_specs=at_slot,
    )
    return pl.pallas_call(
        add_kernel,
        name=f"add{which}",
        out_shape=jax.ShapeDtypeStruct(update.shape, jnp.float32),
        grid_spec=grid,
        input_output_aliases={1: 0},
        compiler_params=params(),
        cost_estimate=SMALL,
    )(idx, update, came)


def route(move, keep=lambda x: True):
    pairs = []
    for x in range(4):
        if keep(x):
            for z in range(4):
                for c in range(2):
                    tx, tz, tc = move(x, z, c)
                    pairs.append(((x * 4 + z) * 2 + c, (tx * 4 + tz) * 2 + tc))
    return pairs


OPPOSITE = route(lambda x, z, c: ((x + 2) % 4, z, c))
SIDE = route(lambda x, z, c: (1 - x, z, c), lambda x: x < 2)
BACK = route(lambda x, z, c: (3 - x, z, c), lambda x: x < 2)
ACROSS = route(lambda x, z, c: (x + 2, z, c), lambda x: x < 2)
Z_UP = route(lambda x, z, c: (x, (z + 1) % 4, c))
Z_DOWN = route(lambda x, z, c: (x, (z + 3) % 4, c))
Z_FAR = route(lambda x, z, c: (x, (z + 2) % 4, c))
CORE = route(lambda x, z, c: (x, z, 1 - c))


def send(value, pairs):
    return lax.ppermute(value, "sub", pairs)


def per_device(front, children, row_maps):
    half = lax.axis_size("sub") // 2
    columns = front.shape[2]
    x = lax.axis_index("sub") // 8

    idx, first, b0, second, base_lead = make_indices(row_maps, front, children, half)
    came_first = send(first, OPPOSITE)
    came_others = send(second, OPPOSITE)
    b1, b2 = take_blocks(idx, children)
    came = [send(b, OPPOSITE) for b in (b0, b1, b2)]

    lead = base_lead + came_first
    side, back, across = send(lead, SIDE), send(lead, BACK), send(lead, ACROSS)
    row_a = jnp.where(x == 0, lead, jnp.where(x == 1, side, jnp.where(x == 2, across, back)))
    row_b = jnp.where(x == 1, lead, jnp.where(x == 0, side, jnp.where(x == 3, across, back)))
    own = jnp.stack([row_a, row_b])

    by_z = [own, send(own, Z_DOWN), send(own, Z_FAR), send(own, Z_UP)]
    pieces = []
    for v in by_z:
        pieces += [v, send(v, CORE)]
    inv, wide = factor(pieces, half, columns)

    panel, update = make_base(idx, front, children, came_first, came_others, inv, wide)
    for which, block in enumerate(came):
        update = add_block(idx, update, block, which)
    return panel, update


def solution(mesh):
    placed = (P("front", "sub", None), P("front", "sub", None), P("front", None))
    return jax.shard_map(
        per_device,
        mesh=mesh,
        in_specs=placed,
        out_specs=(P("front", "sub", None), P("front", "sub", None)),
        check_vma=False,
    )
```

```python
import functools

import jax
import jax.numpy as jnp
from jax import lax
from jax.experimental import pallas as pl
from jax.experimental.pallas import tpu as pltpu
from jax.sharding import PartitionSpec as P

PANEL = 256
BLK = 128
LANES = 128
HIGHEST = lax.Precision.HIGHEST
VMEM_LIMIT = 60 << 20
GROUP = 64
HEAD = 1152
CHUNKS = ((0, 0, HEAD), (1, 256, 1792), (2, 256, 1792), (0, HEAD, 896))

OUT = 0
SLOT = 4
KEEP = 8
CAME = 12
SMALL = pl.CostEstimate(flops=0, bytes_accessed=0, transcendentals=0)


def matmul(a, b, ca, cb):
    return lax.dot_general(
        a, b, (((ca,), (cb,)), ((), ())), precision=HIGHEST, preferred_element_type=jnp.float32
    )


def split(a):
    parts = []
    for _ in range(3):
        parts.append(a.astype(jnp.bfloat16))
        a = a - parts[-1].astype(jnp.float32)
    return parts


def any_space():
    return pl.BlockSpec(memory_space=pl.ANY)


def smem_space():
    return pl.BlockSpec(memory_space=pltpu.SMEM)


def params():
    return pltpu.CompilerParams(vmem_limit_bytes=VMEM_LIMIT)


def index_kernel(half, slots, maps, front, children, idx, piece, others, mine, theirs, old, kept, sent, sem):
    dev = lax.axis_index("sub")
    sib = dev // half
    res = dev % half
    lead = pl.ds(0, PANEL)
    first = pltpu.make_async_copy(front.at[0, :, lead], old, sem.at[0])
    first.start()
    for step in range(8):
        mine[step] = -1
        theirs[step] = -1
    for b in range(slots):
        mine[(maps[sib, b * half + res] - res) // half] = b
        theirs[(maps[1 - sib, b * half + res] - res) // half] = b
    for i in range(16):
        idx[i] = -1
    n_out = jnp.int32(0)
    n_in = jnp.int32(0)
    none = jnp.int32(0)
    for q in range(4):
        b = mine[2 * q + 1 - sib]
        idx[OUT + n_out] = jnp.maximum(b, 0)
        n_out = n_out + jnp.where(b >= 0, 1, 0)
        idx[KEEP + q] = mine[2 * q + sib]
        t = theirs[2 * q + sib]
        idx[SLOT + n_in] = q
        idx[CAME + q] = jnp.where(t >= 0, n_in, -1)
        n_in = n_in + jnp.where(t >= 0, 1, 0)
        none = jnp.where(t >= 0, none, q)
    idx[SLOT + 3] = none
    keep = idx[KEEP]
    copies = [
        pltpu.make_async_copy(children.at[jnp.maximum(keep, 0), :, lead], kept, sem.at[1])
    ] + [
        pltpu.make_async_copy(children.at[idx[OUT + i], :, lead], out, sem.at[2 + i])
        for i, out in enumerate((sent, others.at[0], others.at[1]))
    ]
    for copy in copies:
        copy.start()
    first.wait()
    for copy in copies:
        copy.wait()
    mine_at_0 = old[...] + kept[...] * jnp.where(keep >= 0, 1.0, 0.0)
    piece[...] = jnp.where(sib == 0, mine_at_0, sent[...])


def make_indices(row_maps, front, children, half):
    vmem = pl.BlockSpec(memory_space=pltpu.VMEM)
    return pl.pallas_call(
        functools.partial(index_kernel, half, children.shape[0]),
        name="indices",
        out_shape=(
            jax.ShapeDtypeStruct((16,), jnp.int32),
            jax.ShapeDtypeStruct((BLK, PANEL), jnp.float32),
            jax.ShapeDtypeStruct((2, BLK, PANEL), jnp.float32),
        ),
        in_specs=[smem_space(), any_space(), any_space()],
        out_specs=(smem_space(), vmem, vmem),
        scratch_shapes=[
            pltpu.SMEM((8,), jnp.int32),
            pltpu.SMEM((8,), jnp.int32),
            pltpu.VMEM((BLK, PANEL), jnp.float32),
            pltpu.VMEM((BLK, PANEL), jnp.float32),
            pltpu.VMEM((BLK, PANEL), jnp.float32),
            pltpu.SemaphoreType.DMA((5,)),
        ],
        compiler_params=params(),
        cost_estimate=SMALL,
    )(row_maps, front, children)


def take_kernel(idx, children, *refs):
    outs, sem = refs[:-1], refs[-1]
    copies = []
    for i, (out, (which, low, width)) in enumerate(zip(outs, CHUNKS)):
        part = pl.ds(low, width)
        copies.append(pltpu.make_async_copy(children.at[idx[OUT + which], :, part], out, sem.at[i]))
    for copy in copies:
        copy.start()
    for copy in copies:
        copy.wait()


def take_blocks(idx, children):
    vmem = pl.BlockSpec(memory_space=pltpu.VMEM)
    return pl.pallas_call(
        take_kernel,
        name="take",
        out_shape=[jax.ShapeDtypeStruct((BLK, width), jnp.float32) for _, _, width in CHUNKS],
        in_specs=[smem_space(), any_space()],
        out_specs=[vmem for _ in CHUNKS],
        scratch_shapes=[pltpu.SemaphoreType.DMA((len(CHUNKS),))],
        compiler_params=params(),
        cost_estimate=SMALL,
    )(idx, children)


def lead_kernel(n, *refs):
    refs[2 + n][...] = refs[0][...] + refs[1][...]


def lead_piece(piece, came, later):
    vmem = pl.BlockSpec(memory_space=pltpu.VMEM)
    n = len(later)
    out = pl.pallas_call(
        functools.partial(lead_kernel, n),
        name="lead",
        out_shape=[jax.ShapeDtypeStruct((BLK, PANEL), jnp.float32)]
        + [jax.ShapeDtypeStruct(b.shape, b.dtype) for b in later],
        in_specs=[vmem, vmem] + [any_space() for _ in later],
        out_specs=[vmem] + [any_space() for _ in later],
        input_output_aliases={2 + i: 1 + i for i in range(n)},
        compiler_params=params(),
        cost_estimate=SMALL,
    )(piece, came, *later)
    return out[0], list(out[1:])


def pair_kernel(*refs):
    refs[-1][0] = refs[0][...]
    refs[-1][1] = refs[1][...]


def pair(one, two, *after):
    vmem = pl.BlockSpec(memory_space=pltpu.VMEM)
    return pl.pallas_call(
        pair_kernel,
        name="pair",
        out_shape=jax.ShapeDtypeStruct((2, BLK, PANEL), jnp.float32),
        in_specs=[vmem] * 2 + [any_space() for _ in after],
        out_specs=vmem,
        compiler_params=params(),
        cost_estimate=SMALL,
    )(one, two, *after)


def inverse_factor(d):
    n = d.shape[0]
    row = lax.broadcasted_iota(jnp.int32, (n, n), 0)
    col = lax.broadcasted_iota(jnp.int32, (n, n), 1)
    m = jnp.concatenate([d, (row == col).astype(jnp.float32)], axis=1)
    w = 2 * n
    parts = n // 8
    groups = [m[8 * i : 8 * i + 8, :] for i in range(parts)]
    sub = lax.broadcasted_iota(jnp.int32, (8, w), 0)
    for q in range(parts):
        e = [
            [
                jnp.broadcast_to(groups[i][:, 8 * q + k : 8 * q + k + 1], (8, w))
                for i in range(q, parts)
            ]
            for k in range(8)
        ]
        for k in range(8):
            r = lax.rsqrt(jnp.broadcast_to(e[k][0][k : k + 1, :], (8, w)))
            pivot_row = jnp.broadcast_to(groups[q][k : k + 1, :], (8, w)) * r
            scaled = [v * r for v in e[k]]
            for i in range(q, parts):
                t = groups[i] - scaled[i - q] * pivot_row
                if i == q:
                    t = jnp.where(sub == k, pivot_row, jnp.where(sub > k, t, groups[i]))
                groups[i] = t
            for c in range(k + 1, 8):
                head = jnp.broadcast_to(e[c][0][k : k + 1, :], (8, w)) * r
                e[c] = [v - u * head for v, u in zip(e[c], scaled)]
    return jnp.concatenate(groups, axis=0)[:, n:]


def factor_kernel(half, *refs):
    pieces, (inv, wide, window, m) = refs[:8], refs[-4:]
    dev = lax.axis_index("sub")
    h0 = (dev // 8) % 2
    z = (dev // 2) % 4
    core = dev % 2
    for i, ref in enumerate(pieces):
        zz = (z + i // 2) % 4
        cc = (core + i) % 2
        for h in range(2):
            block = ((h0 + h) % 2 * 4 + zz) * 2 + cc
            window[pl.ds(pl.multiple_of(block * BLK, BLK), BLK), :] = ref[h]
    s = window[0:PANEL, :]
    s = 0.5 * (s + s.T)
    m[:, :PANEL] = s
    row = lax.broadcasted_iota(jnp.int32, (PANEL, PANEL), 0)
    col = lax.broadcasted_iota(jnp.int32, (PANEL, PANEL), 1)
    m[:, PANEL:] = (row == col).astype(jnp.float32)
    for k in range(PANEL // GROUP):
        a, b = k * GROUP, (k + 1) * GROUP
        r = m[a:b, :]
        x = matmul(inverse_factor(r[:, a:b]), r, 1, 0)
        m[a:b, :] = x
        if b < PANEL:
            m[b:, :] = m[b:, :] - matmul(x[:, b:PANEL], x, 0, 0)
    linv = m[:, PANEL:]
    inv[...] = linv
    wide[...] = jnp.concatenate(split(matmul(window[PANEL:, :], linv, 1, 1)), axis=1)


def factor(pieces, half, columns, *after):
    return pl.pallas_call(
        functools.partial(factor_kernel, half),
        name="factor",
        out_shape=(
            jax.ShapeDtypeStruct((PANEL, PANEL), jnp.float32),
            jax.ShapeDtypeStruct((columns - PANEL, 3 * PANEL), jnp.bfloat16),
        ),
        in_specs=[pl.BlockSpec(memory_space=pltpu.VMEM)] * 8 + [any_space() for _ in after],
        scratch_shapes=[
            pltpu.VMEM((columns, PANEL), jnp.float32),
            pltpu.VMEM((PANEL, 2 * PANEL), jnp.float32),
        ],
        compiler_params=params(),
        cost_estimate=SMALL,
    )(*pieces, *after)


def base_kernel(slots, idx, *refs):
    fronts, lead_front, refs = refs[0], refs[1], refs[2:]
    kept, lead_kept, (others, head, inv, wide, *_, panel, update, held) = (
        refs[:slots], refs[slots : 2 * slots], refs[2 * slots :]
    )
    has = [jnp.where(idx[KEEP + q] >= 0, 1.0, 0.0) for q in range(slots)]

    @pl.when(pl.program_id(0) == 0)
    def _():
        for q in range(slots):
            which = idx[CAME + q]
            second = others[jnp.clip(which - 1, 0, 1)] * jnp.where(which >= 0, 1.0, 0.0)
            got = jnp.where(which == 0, head[:, :PANEL], second)
            panel[q] = lead_front[q] + lead_kept[q][0] * has[q] + got
        p = matmul(panel[...].reshape(slots * BLK, PANEL), inv[...], 1, 1)
        panel[...] = p.reshape(slots, BLK, PANEL)
        a, b, c = split(p)
        for i, part in enumerate((a, a, b, b, a, c)):
            held[:, i * PANEL : (i + 1) * PANEL] = part

    def block0(part):
        at = PANEL + pl.program_id(0) * PANEL + part * LANES
        first = pl.multiple_of(jnp.minimum(at, HEAD - LANES), LANES)
        return head[:, pl.ds(first, LANES)] * jnp.where(at < HEAD, 1.0, 0.0)

    a, b, c = (wide[:, i * PANEL : (i + 1) * PANEL] for i in range(3))
    u = lax.dot_general(
        held[...],
        jnp.concatenate([a, b, a, b, c, a], axis=1),
        (((1,), (1,)), ((), ())),
        preferred_element_type=jnp.float32,
    )
    for q in range(slots):
        new = fronts[q] + kept[q][0] * has[q] - u[q * BLK : (q + 1) * BLK, :]
        if q == 0:
            new = new + jnp.concatenate([block0(0), block0(1)], axis=1)
        update[q] = new


def make_base(idx, front, children, others, head, inv, wide, *after):
    slots, rows, columns = front.shape
    rest = columns - PANEL
    whole = lambda shape: pl.BlockSpec(shape, lambda i, idx: (0,) * len(shape))
    kept = lambda q, at: pl.BlockSpec(
        (1, rows, PANEL), lambda i, idx: (jnp.maximum(idx[KEEP + q], 0), 0, (i + 1) * at)
    )
    in_specs = (
        [
            pl.BlockSpec((slots, rows, PANEL), lambda i, idx: (0, 0, i + 1)),
            pl.BlockSpec((slots, rows, PANEL), lambda i, idx: (0, 0, 0)),
        ]
        + [kept(q, 1) for q in range(slots)]
        + [kept(q, 0) for q in range(slots)]
        + [
            whole(others.shape),
            whole(head.shape),
            whole(inv.shape),
            pl.BlockSpec((PANEL, 3 * PANEL), lambda i, idx: (i, 0)),
        ]
        + [any_space() for _ in after]
    )
    grid = pltpu.PrefetchScalarGridSpec(
        num_scalar_prefetch=1,
        grid=(rest // PANEL,),
        in_specs=in_specs,
        out_specs=(
            whole((slots, rows, PANEL)),
            pl.BlockSpec((slots, rows, PANEL), lambda i, idx: (0, 0, i)),
        ),
        scratch_shapes=[pltpu.VMEM((slots * rows, 6 * PANEL), jnp.bfloat16)],
    )
    return pl.pallas_call(
        functools.partial(base_kernel, slots),
        name="base",
        out_shape=(
            jax.ShapeDtypeStruct((slots, rows, PANEL), jnp.float32),
            jax.ShapeDtypeStruct((slots, rows, rest), jnp.float32),
        ),
        grid_spec=grid,
        compiler_params=params(),
        cost_estimate=SMALL,
    )(idx, *[front] * 2, *[children] * (2 * slots), others, head, inv, wide, *after)


def add_kernel(idx, old, came, out):
    out[0] = old[0] + came[...]


def add_block(idx, update, came, which):
    slots, rows, rest = update.shape
    block, low, width = CHUNKS[which]
    at_slot = pl.BlockSpec(
        (1, rows, width), lambda i, idx: (idx[SLOT + block], 0, (low - PANEL) // width)
    )
    grid = pltpu.PrefetchScalarGridSpec(
        num_scalar_prefetch=1,
        grid=(1,),
        in_specs=[at_slot, pl.BlockSpec(came.shape, lambda i, idx: (0, 0))],
        out_specs=at_slot,
    )
    return pl.pallas_call(
        add_kernel,
        name=f"add{which}",
        out_shape=jax.ShapeDtypeStruct(update.shape, jnp.float32),
        grid_spec=grid,
        input_output_aliases={1: 0},
        compiler_params=params(),
        cost_estimate=SMALL,
    )(idx, update, came)


def route(move, keep=lambda x: True):
    pairs = []
    for x in range(4):
        if keep(x):
            for z in range(4):
                for c in range(2):
                    tx, tz, tc = move(x, z, c)
                    pairs.append(((x * 4 + z) * 2 + c, (tx * 4 + tz) * 2 + tc))
    return pairs


OPPOSITE = route(lambda x, z, c: ((x + 2) % 4, z, c))
SIDE = route(lambda x, z, c: (x ^ 1, z, c))
Z_UP = route(lambda x, z, c: (x, (z + 1) % 4, c))
Z_DOWN = route(lambda x, z, c: (x, (z + 3) % 4, c))
Z_FAR = route(lambda x, z, c: (x, (z + 2) % 4, c))
CORE = route(lambda x, z, c: (x, z, 1 - c))


def send(value, pairs):
    return lax.ppermute(value, "sub", pairs)


def per_device(front, children, row_maps):
    half = lax.axis_size("sub") // 2
    columns = front.shape[2]

    idx, piece, panels = make_indices(row_maps, front, children, half)
    came_piece = send(piece, OPPOSITE)
    blocks = take_blocks(idx, children)
    came_panels = send(panels, OPPOSITE)

    lead, blocks = lead_piece(piece, came_piece, blocks)
    came = [send(b, OPPOSITE) for b in blocks]
    own = pair(lead, send(lead, SIDE), came_panels)

    by_z = [own, send(own, Z_DOWN), send(own, Z_FAR), send(own, Z_UP)]
    *by_z, came[0] = lax.optimization_barrier((*by_z, came[0]))
    pieces = []
    for v in by_z:
        pieces += [v, send(v, CORE)]
    inv, wide = factor(pieces, half, columns)

    panel, update = make_base(idx, front, children, came_panels, came[0], inv, wide)
    for which in range(1, len(CHUNKS)):
        update = add_block(idx, update, came[which], which)
    return panel, update


def solution(mesh):
    placed = (P("front", "sub", None), P("front", "sub", None), P("front", None))
    return jax.shard_map(
        per_device,
        mesh=mesh,
        in_specs=placed,
        out_specs=(P("front", "sub", None), P("front", "sub", None)),
        check_vma=False,
    )
```

```python
import functools

import jax
import jax.numpy as jnp
from jax import lax
from jax.experimental import pallas as pl
from jax.experimental.pallas import tpu as pltpu
from jax.sharding import PartitionSpec as P

PANEL = 256
BLK = 128
LANES = 128
HIGHEST = lax.Precision.HIGHEST
VMEM_LIMIT = 60 << 20
GROUP = 64
HEAD = 896
CHUNKS = ((0, 256, HEAD), (1, 256, 1792), (2, 256, 1792), (0, 256 + HEAD, 1792 - HEAD))

OUT = 0
SLOT = 4
KEEP = 8
CAME = 12
SMALL = pl.CostEstimate(flops=0, bytes_accessed=0, transcendentals=0)


def matmul(a, b, ca, cb):
    return lax.dot_general(
        a, b, (((ca,), (cb,)), ((), ())), precision=HIGHEST, preferred_element_type=jnp.float32
    )


def split(a):
    parts = []
    for _ in range(3):
        parts.append(a.astype(jnp.bfloat16))
        a = a - parts[-1].astype(jnp.float32)
    return parts


def any_space():
    return pl.BlockSpec(memory_space=pl.ANY)


def smem_space():
    return pl.BlockSpec(memory_space=pltpu.SMEM)


def params():
    return pltpu.CompilerParams(vmem_limit_bytes=VMEM_LIMIT)


def index_kernel(half, slots, maps, front, children, idx, piece, others, mine, theirs, old, kept, sem):
    dev = lax.axis_index("sub")
    sib = dev // half
    res = dev % half
    lead = pl.ds(0, PANEL)
    first = pltpu.make_async_copy(front.at[0, :, lead], old, sem.at[0])
    first.start()
    for step in range(8):
        mine[step] = -1
        theirs[step] = -1
    for b in range(slots):
        mine[(maps[sib, b * half + res] - res) // half] = b
        theirs[(maps[1 - sib, b * half + res] - res) // half] = b
    for i in range(16):
        idx[i] = -1
    n_out = jnp.int32(0)
    n_in = jnp.int32(0)
    none = jnp.int32(0)
    for q in range(4):
        b = mine[2 * q + 1 - sib]
        idx[OUT + n_out] = jnp.maximum(b, 0)
        n_out = n_out + jnp.where(b >= 0, 1, 0)
        idx[KEEP + q] = mine[2 * q + sib]
        t = theirs[2 * q + sib]
        idx[SLOT + n_in] = q
        idx[CAME + q] = jnp.where(t >= 0, n_in, -1)
        n_in = n_in + jnp.where(t >= 0, 1, 0)
        none = jnp.where(t >= 0, none, q)
    idx[SLOT + 3] = none
    keep = idx[KEEP]
    copies = [
        pltpu.make_async_copy(children.at[jnp.maximum(keep, 0), :, lead], kept, sem.at[1])
    ] + [
        pltpu.make_async_copy(children.at[idx[OUT + i], :, lead], out, sem.at[2 + i])
        for i, out in enumerate((others.at[0], others.at[1], others.at[2]))
    ]
    for copy in copies:
        copy.start()
    first.wait()
    for copy in copies:
        copy.wait()
    mine_at_0 = old[...] + kept[...] * jnp.where(keep >= 0, 1.0, 0.0)
    piece[...] = jnp.where(sib == 0, mine_at_0, others[0])


def make_indices(row_maps, front, children, half):
    vmem = pl.BlockSpec(memory_space=pltpu.VMEM)
    return pl.pallas_call(
        functools.partial(index_kernel, half, children.shape[0]),
        name="indices",
        out_shape=(
            jax.ShapeDtypeStruct((16,), jnp.int32),
            jax.ShapeDtypeStruct((BLK, PANEL), jnp.float32),
            jax.ShapeDtypeStruct((3, BLK, PANEL), jnp.float32),
        ),
        in_specs=[smem_space(), any_space(), any_space()],
        out_specs=(smem_space(), vmem, vmem),
        scratch_shapes=[
            pltpu.SMEM((8,), jnp.int32),
            pltpu.SMEM((8,), jnp.int32),
            pltpu.VMEM((BLK, PANEL), jnp.float32),
            pltpu.VMEM((BLK, PANEL), jnp.float32),
            pltpu.SemaphoreType.DMA((5,)),
        ],
        compiler_params=params(),
        cost_estimate=SMALL,
    )(row_maps, front, children)


def take_kernel(idx, children, *refs):
    outs, sem = refs[:-1], refs[-1]
    copies = []
    for i, (out, (which, low, width)) in enumerate(zip(outs, CHUNKS)):
        part = pl.ds(low, width)
        copies.append(pltpu.make_async_copy(children.at[idx[OUT + which], :, part], out, sem.at[i]))
    for copy in copies:
        copy.start()
    for copy in copies:
        copy.wait()


def take_blocks(idx, children):
    vmem = pl.BlockSpec(memory_space=pltpu.VMEM)
    return pl.pallas_call(
        take_kernel,
        name="take",
        out_shape=[jax.ShapeDtypeStruct((BLK, width), jnp.float32) for _, _, width in CHUNKS],
        in_specs=[smem_space(), any_space()],
        out_specs=[vmem for _ in CHUNKS],
        scratch_shapes=[pltpu.SemaphoreType.DMA((len(CHUNKS),))],
        compiler_params=params(),
        cost_estimate=SMALL,
    )(idx, children)


def inverse_factor(d):
    n = d.shape[0]
    row = lax.broadcasted_iota(jnp.int32, (n, n), 0)
    col = lax.broadcasted_iota(jnp.int32, (n, n), 1)
    m = jnp.concatenate([d, (row == col).astype(jnp.float32)], axis=1)
    w = 2 * n
    parts = n // 8
    groups = [m[8 * i : 8 * i + 8, :] for i in range(parts)]
    sub = lax.broadcasted_iota(jnp.int32, (8, w), 0)
    for q in range(parts):
        e = [
            [
                jnp.broadcast_to(groups[i][:, 8 * q + k : 8 * q + k + 1], (8, w))
                for i in range(q, parts)
            ]
            for k in range(8)
        ]
        for k in range(8):
            r = lax.rsqrt(jnp.broadcast_to(e[k][0][k : k + 1, :], (8, w)))
            pivot_row = jnp.broadcast_to(groups[q][k : k + 1, :], (8, w)) * r
            scaled = [v * r for v in e[k]]
            for i in range(q, parts):
                t = groups[i] - scaled[i - q] * pivot_row
                if i == q:
                    t = jnp.where(sub == k, pivot_row, jnp.where(sub > k, t, groups[i]))
                groups[i] = t
            for c in range(k + 1, 8):
                head = jnp.broadcast_to(e[c][0][k : k + 1, :], (8, w)) * r
                e[c] = [v - u * head for v, u in zip(e[c], scaled)]
    return jnp.concatenate(groups, axis=0)[:, n:]


def main_kernel(half, idx, *refs):
    pieces, (front, children, others, head), refs = refs[:8], refs[8:12], refs[12:]
    panel, update, window, m, base, kept, got, first, held, stage, sem = refs
    slots = base.shape[0]
    tiles = update.shape[2] // PANEL
    loads = [pltpu.make_async_copy(front, base, sem.at[0])]
    loads += [
        pltpu.make_async_copy(children.at[jnp.maximum(idx[KEEP + q], 0)], kept.at[q], sem.at[1 + q])
        for q in range(slots)
    ]
    loads += [
        pltpu.make_async_copy(others, got, sem.at[slots + 1]),
        pltpu.make_async_copy(head, first, sem.at[slots + 2]),
    ]
    for load in loads:
        load.start()

    dev = lax.axis_index("sub")
    h0 = (dev // 8) % 2
    z = (dev // 2) % 4
    core = dev % 2
    for i, ref in enumerate(pieces):
        zz = (z + i // 2) % 4
        cc = (core + i) % 2
        for h in range(2):
            block = ((h0 + h) % 2 * 4 + zz) * 2 + cc
            window[pl.ds(pl.multiple_of(block * BLK, BLK), BLK), :] = ref[h]
    s = window[0:PANEL, :]
    s = 0.5 * (s + s.T)
    m[:, :PANEL] = s
    row = lax.broadcasted_iota(jnp.int32, (PANEL, PANEL), 0)
    col = lax.broadcasted_iota(jnp.int32, (PANEL, PANEL), 1)
    m[:, PANEL:] = (row == col).astype(jnp.float32)
    for k in range(PANEL // GROUP):
        a, b = k * GROUP, (k + 1) * GROUP
        r = m[a:b, :]
        x = matmul(inverse_factor(r[:, a:b]), r, 1, 0)
        m[a:b, :] = x
        if b < PANEL:
            m[b:, :] = m[b:, :] - matmul(x[:, b:PANEL], x, 0, 0)

    for load in loads:
        load.wait()
    has = [jnp.where(idx[KEEP + q] >= 0, 1.0, 0.0) for q in range(slots)]
    leads = []
    for q in range(slots):
        which = idx[CAME + q]
        block = got[jnp.maximum(which, 0)] * jnp.where(which >= 0, 1.0, 0.0)
        leads.append(base[q, :, :PANEL] + kept[q, :, :PANEL] * has[q] + block)
    p = matmul(jnp.concatenate(leads, axis=0), m[:, PANEL:], 1, 1)
    stage[...] = p.reshape(stage.shape)
    saves = [pltpu.make_async_copy(stage, panel, sem.at[0])]
    saves[0].start()
    a, b, c = split(p)
    for i, part in enumerate((a, a, b, b, a, c)):
        held[:, i * PANEL : (i + 1) * PANEL] = part

    for t in range(tiles):
        low = PANEL * (t + 1)
        cols = slice(low, low + PANEL)
        a, b, c = split(matmul(window[cols, :], m[:, PANEL:], 1, 1))
        u = lax.dot_general(
            held[...],
            jnp.concatenate([a, b, a, b, c, a], axis=1),
            (((1,), (1,)), ((), ())),
            preferred_element_type=jnp.float32,
        )
        for q in range(slots):
            base[q, :, cols] = (
                base[q, :, cols] + kept[q, :, cols] * has[q] - u[q * BLK : (q + 1) * BLK, :]
            )
        width = min(max(HEAD + PANEL - low, 0), PANEL)
        if width:
            part = slice(low, low + width)
            base[0, :, part] = base[0, :, part] + first[:, low - PANEL : low - PANEL + width]
        saves.append(
            pltpu.make_async_copy(
                base.at[:, :, pl.ds(low, PANEL)],
                update.at[:, :, pl.ds(low - PANEL, PANEL)],
                sem.at[1 + t],
            )
        )
        saves[-1].start()
    for save in saves:
        save.wait()


def main(idx, pieces, front, children, others, head, half):
    slots, rows, columns = front.shape
    rest = columns - PANEL
    f32 = jnp.float32
    hbm = pl.BlockSpec(memory_space=pltpu.HBM)
    return pl.pallas_call(
        functools.partial(main_kernel, half),
        name="main",
        out_shape=(
            jax.ShapeDtypeStruct((slots, rows, PANEL), f32),
            jax.ShapeDtypeStruct((slots, rows, rest), f32),
        ),
        in_specs=[smem_space()]
        + [pl.BlockSpec(memory_space=pltpu.VMEM)] * 8
        + [hbm] * 4,
        out_specs=(hbm, hbm),
        scratch_shapes=[
            pltpu.VMEM((columns, PANEL), f32),
            pltpu.VMEM((PANEL, 2 * PANEL), f32),
            pltpu.VMEM((slots, rows, columns), f32),
            pltpu.VMEM((slots, rows, columns), f32),
            pltpu.VMEM(others.shape, f32),
            pltpu.VMEM(head.shape, f32),
            pltpu.VMEM((slots * rows, 6 * PANEL), jnp.bfloat16),
            pltpu.VMEM((slots, rows, PANEL), f32),
            pltpu.SemaphoreType.DMA((8,)),
        ],
        compiler_params=params(),
        cost_estimate=SMALL,
    )(idx, *pieces, front, children, others, head)


def add_block(idx, update, came, which):
    block, low, width = CHUNKS[which]
    at = (idx[SLOT + block], 0, low - PANEL)
    old = lax.dynamic_slice(update, at, (1, BLK, width))
    return lax.dynamic_update_slice(update, old + came[None], at)


def route(move, keep=lambda x: True):
    pairs = []
    for x in range(4):
        if keep(x):
            for z in range(4):
                for c in range(2):
                    tx, tz, tc = move(x, z, c)
                    pairs.append(((x * 4 + z) * 2 + c, (tx * 4 + tz) * 2 + tc))
    return pairs


OPPOSITE = route(lambda x, z, c: ((x + 2) % 4, z, c))
X_UP = route(lambda x, z, c: ((x + 1) % 4, z, c))
X_DOWN = route(lambda x, z, c: ((x + 3) % 4, z, c))
Z_UP = route(lambda x, z, c: (x, (z + 1) % 4, c))
Z_DOWN = route(lambda x, z, c: (x, (z + 3) % 4, c))
Z_FAR = route(lambda x, z, c: (x, (z + 2) % 4, c))
CORE = route(lambda x, z, c: (x, z, 1 - c))


def send(value, pairs):
    return lax.ppermute(value, "sub", pairs)


def per_device(front, children, row_maps):
    half = lax.axis_size("sub") // 2
    columns = front.shape[2]

    idx, piece, panels = make_indices(row_maps, front, children, half)
    came_piece = send(piece, OPPOSITE)
    blocks = take_blocks(idx, children)
    came_panels = send(panels, OPPOSITE)

    came_piece, *blocks = lax.optimization_barrier((came_piece, *blocks))
    lead = piece + came_piece
    came = [send(b, OPPOSITE) for b in blocks]
    above = send(lead[: BLK // 2], X_UP)
    below = send(lead[BLK // 2 :], X_DOWN)
    own = jnp.stack([lead, jnp.concatenate([above, below])])
    own, came_panels = lax.optimization_barrier((own, came_panels))

    by_z = [own, send(own, Z_DOWN), send(own, Z_FAR), send(own, Z_UP)]
    *by_z, came[0] = lax.optimization_barrier((*by_z, came[0]))
    pieces = []
    for v in by_z:
        pieces += [v, send(v, CORE)]
    panel, update = main(idx, pieces, front, children, came_panels, came[0], half)
    for which in range(1, len(CHUNKS)):
        update = add_block(idx, update, came[which], which)
    return panel, update


def solution(mesh):
    placed = (P("front", "sub", None), P("front", "sub", None), P("front", None))
    return jax.shard_map(
        per_device,
        mesh=mesh,
        in_specs=placed,
        out_specs=(P("front", "sub", None), P("front", "sub", None)),
        check_vma=False,
    )
```
